32 devices in a mesh: seq: 16 (over z, y, core), head: 2 (over x).
Axes of the slice: x: 2, y: 2, z: 4, core: 2. Of those that a mesh axis runs over, the one named last changes fastest.
Arguments:
- fast_q: bfloat16 [4096, 4096], P('seq', 'head'), may hold values from -6 to 6
- fast_k: bfloat16 [4096, 4096], P('seq', 'head'), may hold values from -6 to 6
- fast_v: bfloat16 [4096, 4096], P('seq', 'head'), may hold values from -6 to 6
- rates: float32 [8, 4096], P('head', 'seq'), may hold values from 0.02 to 1
- w_gate: bfloat16 [8, 512, 512], P('head'), may hold values from -0.25 to 0.25
- w_up: bfloat16 [8, 512, 512], P('head'), may hold values from -0.25 to 0.25
- w_down: bfloat16 [8, 512, 512], P('head'), may hold values from -0.25 to 0.25
- w_out: bfloat16 [4096, 5120], P('head'), may hold values from -0.09375 to 0.09375
- att_q: bfloat16 [4096, 5120], P('seq', 'head'), may hold values from -5 to 5
- att_k: bfloat16 [4096, 5120], P('seq', 'head'), may hold values from -5 to 5
- att_v: bfloat16 [4096, 5120], P('seq', 'head'), may hold values from -6 to 6
Outputs:
- mixed: bfloat16 [4096, 5120], P('seq', 'head')
- final_weights: bfloat16 [3, 8, 512, 512], P(None, 'head', 'seq')
The draws below stay inside these ranges and needn't reach their ends.
All inputs are finite; a program needn't handle non-finite values.
Results may differ from the reference program's by a relative error of at most 0.022.
Values may be sent and summed in bfloat16 or wider, within the bound.
A program may use at most 128 MiB of HBM per device.

```python
import math
import jax
import jax.numpy as jnp
from jax import lax

HEADS = 8
DH = 512
AHEADS = 40
AD = 128
SPANS = 2
NS_STEPS = 2
TOK_DEV = 256
D = 5120
TOKENS = 4096
WINDOW = 256
N_HEAD = 2


def attention_pair(key):
    base = jax.random.fold_in(key, 4242)
    queries = jnp.clip(1.5 * jax.random.normal(jax.random.fold_in(base, 1), (TOKENS, D), jnp.float32), -5.0, 5.0)
    keys_drawn = jnp.clip(1.5 * jax.random.normal(jax.random.fold_in(base, 2), (TOKENS, D), jnp.float32), -5.0, 5.0)
    return (queries, keys_drawn)


def draw_att_q(key, part):
    return attention_pair(key)[0].astype(jnp.bfloat16)


def draw_att_k(key, part):
    return attention_pair(key)[1].astype(jnp.bfloat16)


def levels(rng, extent, cuts, low, high):
    def one(axis_at, shards_of):
        heights = jax.random.uniform(jax.random.fold_in(jax.random.fold_in(rng, 6), axis_at), (shards_of,), jnp.float32, low / len(cuts), high / len(cuts))
        return jnp.repeat(jnp.exp(heights), extent[axis_at] // shards_of).reshape((-1,) + (1,) * (len(extent) - axis_at - 1))

    factor_of = one(*cuts[0])
    for cut in cuts[1:]:
        factor_of = factor_of * one(*cut)
    return factor_of


def noise(own_key, extent, width, limit, cuts=(), held_as=jnp.bfloat16):
    drawn = width * jax.random.normal(own_key, extent, jnp.float32)
    if cuts:
        drawn = drawn * levels(own_key, extent, cuts, -0.22, 0.18)
    return jnp.clip(drawn, -limit, limit).astype(held_as)


def setup_inputs(seed: int = 0) -> dict:
    splits = jax.random.split(jax.random.key(seed), 12)
    fast_q = noise(splits[0], (TOKENS, HEADS * DH), 1.0, 6.0, ((0, 16), (1, 2)))
    fast_k = noise(splits[1], (TOKENS, HEADS * DH), 1.0, 6.0, ((0, 16), (1, 2)))
    fast_v = noise(splits[2], (TOKENS, HEADS * DH), 1.0, 6.0, ((0, 16), (1, 2)))
    rates = jnp.clip(jnp.exp(math.log(1.0) - 3.912023 * jax.random.uniform(splits[3], (HEADS, TOKENS), jnp.float32) ** levels(splits[3], (HEADS, TOKENS), ((0, 2), (1, 16)), -0.2, 0.2)), 0.02, 1.0)
    w_gate = noise(splits[4], (HEADS, DH, DH), DH ** -0.5, 0.25, ((0, 2),))
    w_up = noise(splits[5], (HEADS, DH, DH), DH ** -0.5, 0.25, ((0, 2),))
    w_down = noise(splits[6], (HEADS, DH, DH), DH ** -0.5, 0.25, ((0, 2),))
    w_out = noise(splits[7], (HEADS * DH, D), (HEADS * DH) ** -0.5, 0.09375, ((0, 2),))
    att_q = draw_att_q(jax.random.fold_in(splits[11], 71), 0)
    att_k = draw_att_k(jax.random.fold_in(splits[11], 71), 0)
    att_v = noise(splits[10], (TOKENS, D), 1.0, 6.0, ((0, 16), (1, 2)))
    return {"fast_q": fast_q, "fast_k": fast_k, "fast_v": fast_v, "rates": rates, "w_gate": w_gate, "w_up": w_up, "w_down": w_down, "w_out": w_out, "att_q": att_q, "att_k": att_k, "att_v": att_v}


NEWTON_COEFFS = (3.4445, -4.775, 2.0315)

def silu_slope(values):
    sigmoid_val = jax.nn.sigmoid(values)
    return sigmoid_val * (1.0 + values * (1.0 - sigmoid_val))

def product(pattern, left_op, right_op):
    return jnp.einsum(pattern, left_op.astype(jnp.float32), right_op.astype(jnp.float32))

def fast_apply(weights, queries):
    w_first, w_second, w_third = weights
    gate_pre = product('nhi,hij->nhj', queries, w_first)
    up_pre = product('nhi,hij->nhj', queries, w_second)
    activated = (jax.nn.silu(gate_pre) * up_pre).astype(jnp.bfloat16)
    output = product('nhj,hjk->nhk', activated, w_third)
    factor = lax.rsqrt(lax.optimization_barrier(jnp.mean(output * output, axis=-1, keepdims=True)) + 1e-06)
    return (output * factor).astype(jnp.bfloat16)

def gradients(weights, keys_in, values_in, rate_rows):
    w_first, w_second, w_third = weights
    gate_pre = product('nhi,hij->nhj', keys_in, w_first)
    up_pre = product('nhi,hij->nhj', keys_in, w_second)
    activated = (jax.nn.silu(gate_pre) * up_pre).astype(jnp.bfloat16)
    weighted = (rate_rows[:, :, None] * values_in.astype(jnp.float32)).astype(jnp.bfloat16)
    grad_third = -product('nhj,nhk->hjk', activated, weighted)
    back = -product('nhk,hjk->nhj', weighted, w_third)
    up_in = (back * jax.nn.silu(gate_pre)).astype(jnp.bfloat16)
    gate_in = (back * up_pre * silu_slope(gate_pre)).astype(jnp.bfloat16)
    grad_first = product('nhi,nhj->hij', keys_in, gate_in)
    grad_second = product('nhi,nhj->hij', keys_in, up_in)
    return (grad_first, grad_second, grad_third)

def scale_down(summed):
    squares = lax.optimization_barrier(jnp.sum(summed * summed, axis=(1, 2)))
    return (summed / jnp.sqrt(squares + 1e-06)[:, None, None]).astype(jnp.bfloat16)

def newton_schulz(matrix):
    first, second, third = NEWTON_COEFFS
    for iteration in range(NS_STEPS):
        gram = product('mij,mkj->mik', matrix, matrix).astype(jnp.bfloat16)
        square = product('mij,mjk->mik', gram, gram)
        poly = (second * gram.astype(jnp.float32) + third * square).astype(jnp.bfloat16)
        matrix = (first * matrix.astype(jnp.float32) + product('mij,mjk->mik', poly, matrix)).astype(jnp.bfloat16)
    return matrix

def renorm(weight, ortho):
    unmoved = weight.astype(jnp.float32)
    moved = unmoved - ortho.astype(jnp.float32)
    target = jnp.sqrt(lax.optimization_barrier(jnp.sum(unmoved * unmoved, axis=1, keepdims=True)) + 1e-06)
    current = jnp.sqrt(lax.optimization_barrier(jnp.sum(moved * moved, axis=1, keepdims=True)) + 1e-06)
    return (moved * (target / current)).astype(jnp.bfloat16)

def attend(queries, keys_all, values_all, offset, window):
    block = queries.shape[0]
    scores = product('qhd,khd->hqk', queries, keys_all) * queries.shape[-1] ** (-0.5)
    query_pos = offset + lax.broadcasted_iota(jnp.int32, (block, 2 * block), 0)
    key_pos = offset - block + lax.broadcasted_iota(jnp.int32, (block, 2 * block), 1)
    allowed = (key_pos <= query_pos) & (key_pos > query_pos - window) & (key_pos >= 0)
    scores = jnp.where(allowed[None], scores, -1e+30)
    row_max = lax.optimization_barrier(jnp.max(scores, axis=-1, keepdims=True))
    exp_scores = jnp.exp(scores - row_max)
    probs = (exp_scores / lax.optimization_barrier(jnp.sum(exp_scores, axis=-1, keepdims=True))).astype(jnp.bfloat16)
    return product('hqk,khd->qhd', probs, values_all)

def reference(fast_q, fast_k, fast_v, rates, w_gate, w_up, w_down, w_out, att_q, att_k, att_v):
    length = TOKENS // SPANS
    queries = fast_q.reshape(TOKENS, HEADS, DH)
    keys_fast = fast_k.reshape(TOKENS, HEADS, DH)
    values_fast = fast_v.reshape(TOKENS, HEADS, DH)
    weights = (w_gate, w_up, w_down)
    results = []
    for span in range(SPANS):
        lower = span * length
        upper = lower + length
        results.append(fast_apply(weights, queries[lower:upper]))
        grads = gradients(weights, keys_fast[lower:upper], values_fast[lower:upper], rates[:, lower:upper].T)
        ortho = newton_schulz(scale_down(jnp.concatenate(grads, axis=0)))
        pieces = ortho.reshape(3, HEADS, DH, DH)
        weights = tuple((renorm(weights[member], pieces[member]) for member in range(3)))
    final_weights = jnp.stack(weights, axis=0)
    fast_rows = jnp.concatenate(results, axis=0).reshape(TOKENS, HEADS * DH)
    share = HEADS * DH // N_HEAD
    fast_sum = jnp.zeros((TOKENS, D), jnp.float32)
    for group_id in range(N_HEAD):
        partial_out = jnp.dot(fast_rows[:, group_id * share:(group_id + 1) * share], w_out[group_id * share:(group_id + 1) * share], preferred_element_type=jnp.float32).astype(jnp.bfloat16)
        fast_sum = fast_sum + lax.optimization_barrier(partial_out).astype(jnp.float32)
    queries_att = att_q.reshape(TOKENS, AHEADS, AD)
    padding = jnp.zeros((TOK_DEV, AHEADS, AD), jnp.bfloat16)
    keys_pad = jnp.concatenate([padding, att_k.reshape(TOKENS, AHEADS, AD)], axis=0)
    values_pad = jnp.concatenate([padding, att_v.reshape(TOKENS, AHEADS, AD)], axis=0)

    def one_block(block_id):
        offset = (block_id * TOK_DEV).astype(jnp.int32)
        query_block = lax.dynamic_slice_in_dim(queries_att, offset, TOK_DEV, 0)
        key_block = lax.dynamic_slice_in_dim(keys_pad, offset, 2 * TOK_DEV, 0)
        value_block = lax.dynamic_slice_in_dim(values_pad, offset, 2 * TOK_DEV, 0)
        return attend(query_block, key_block, value_block, offset, WINDOW)
    attended = lax.map(one_block, jnp.arange(TOKENS // TOK_DEV, dtype=jnp.int32))
    attended = attended.reshape(TOKENS, D)
    return ((attended + fast_sum).astype(jnp.bfloat16), final_weights)
```

```python
import functools

import jax
import jax.numpy as jnp
from jax import lax
from jax.experimental import pallas as pl
from jax.experimental.pallas import tpu as pltpu
from jax.sharding import PartitionSpec as P

AD = 128
SPANS = 2
NS_STEPS = 2
MESH = pl.DeviceIdType.MESH
VMEM_LIMIT = 52 * 1024 * 1024
KINDS = 3


NEWTON_COEFFS = (3.4445, -4.775, 2.0315)


def passed_along(block, axis, distance):
    devices = range(lax.axis_size(axis))
    route = [(i - distance, i) for i in devices if i - distance in devices]
    return lax.ppermute(block, axis, route)


def silu_slope(values):
    sigmoid_val = jax.nn.sigmoid(values)
    return sigmoid_val * (1.0 + values * (1.0 - sigmoid_val))


def product(pattern, left_op, right_op):
    return jnp.einsum(pattern, left_op, right_op, preferred_element_type=jnp.float32)


def fast_apply(weights, queries):
    w_first, w_second, w_third = weights
    gate_pre = product("nhi,hij->nhj", queries, w_first)
    up_pre = product("nhi,hij->nhj", queries, w_second)
    activated = (jax.nn.silu(gate_pre) * up_pre).astype(jnp.bfloat16)
    output = product("nhj,hjk->nhk", activated, w_third)
    factor = lax.rsqrt(jnp.mean(output * output, axis=-1, keepdims=True) + 1e-06)
    return (output * factor).astype(jnp.bfloat16)


def gradients(weights, keys_in, values_in, rate_rows):
    w_first, w_second, w_third = weights
    gate_pre = product("nhi,hij->nhj", keys_in, w_first)
    up_pre = product("nhi,hij->nhj", keys_in, w_second)
    activated = (jax.nn.silu(gate_pre) * up_pre).astype(jnp.bfloat16)
    weighted = (rate_rows[:, :, None] * values_in.astype(jnp.float32)).astype(jnp.bfloat16)
    grad_third = -product("nhj,nhk->hjk", activated, weighted)
    back = -product("nhk,hjk->nhj", weighted, w_third)
    up_in = (back * jax.nn.silu(gate_pre)).astype(jnp.bfloat16)
    gate_in = (back * up_pre * silu_slope(gate_pre)).astype(jnp.bfloat16)
    grad_first = product("nhi,nhj->hij", keys_in, gate_in)
    grad_second = product("nhi,nhj->hij", keys_in, up_in)
    return (grad_first, grad_second, grad_third)


def scale_down(summed):
    squares = jnp.sum(summed * summed, axis=(1, 2))
    return (summed / jnp.sqrt(squares + 1e-06)[:, None, None]).astype(jnp.bfloat16)


def newton_schulz(matrix):
    first, second, third = NEWTON_COEFFS
    for iteration in range(NS_STEPS):
        gram = product("mij,mkj->mik", matrix, matrix).astype(jnp.bfloat16)
        square = product("mij,mjk->mik", gram, gram)
        poly = (second * gram.astype(jnp.float32) + third * square).astype(jnp.bfloat16)
        matrix = (
            first * matrix.astype(jnp.float32) + product("mij,mjk->mik", poly, matrix)
        ).astype(jnp.bfloat16)
    return matrix


def renorm(weight, ortho):
    unmoved = weight.astype(jnp.float32)
    moved = unmoved - ortho.astype(jnp.float32)
    target = jnp.sqrt(jnp.sum(unmoved * unmoved, axis=1, keepdims=True) + 1e-06)
    current = jnp.sqrt(jnp.sum(moved * moved, axis=1, keepdims=True) + 1e-06)
    return (moved * (target / current)).astype(jnp.bfloat16)


def attend(queries, keys_all, values_all, offset, window):
    block = queries.shape[0]
    scores = product("qhd,khd->hqk", queries, keys_all) * queries.shape[-1] ** (-0.5)
    query_pos = offset + lax.broadcasted_iota(jnp.int32, (block, 2 * block), 0)
    key_pos = offset - block + lax.broadcasted_iota(jnp.int32, (block, 2 * block), 1)
    allowed = (key_pos <= query_pos) & (key_pos > query_pos - window) & (key_pos >= 0)
    scores = jnp.where(allowed[None], scores, -1e30)
    row_max = jnp.max(scores, axis=-1, keepdims=True)
    exp_scores = jnp.exp(scores - row_max)
    probs = (exp_scores / jnp.sum(exp_scores, axis=-1, keepdims=True)).astype(jnp.bfloat16)
    return product("hqk,khd->qhd", probs, values_all)


def on_device(fast_q, fast_k, fast_v, rates, w_gate, w_up, w_down, w_out, att_q, att_k, att_v):
    row_count = fast_q.shape[0]
    heads_here = w_gate.shape[0]
    feature_count = w_gate.shape[1]
    queries = fast_q.reshape(row_count, heads_here, feature_count)
    keys_fast = fast_k.reshape(row_count, heads_here, feature_count)
    values_fast = fast_v.reshape(row_count, heads_here, feature_count)
    rate_rows = rates.T
    seq_count = lax.axis_size("seq")
    position = lax.axis_index("seq")
    group_id = position // (seq_count // SPANS)
    weights = (w_gate, w_up, w_down)
    chosen = weights
    for span in range(SPANS):
        grads = gradients(weights, keys_fast, values_fast, rate_rows)
        stacked = jnp.concatenate(grads, axis=0)
        stacked = jnp.where(group_id == span, stacked, jnp.zeros_like(stacked))
        summed = lax.psum(stacked.astype(jnp.bfloat16), "seq").astype(jnp.float32)
        start_matrix = scale_down(summed)
        ortho = newton_schulz(start_matrix)
        pieces = ortho.reshape(3, heads_here, feature_count, feature_count)
        weights = tuple((renorm(weights[member], pieces[member]) for member in range(3)))
        if span + 1 < SPANS:
            chosen = tuple(
                (
                    jnp.where(group_id == span + 1, fresh, older)
                    for fresh, older in zip(weights, chosen)
                )
            )
    row_share = feature_count // seq_count
    final_all = jnp.stack(weights, axis=0)
    final_weights = lax.dynamic_slice_in_dim(final_all, position * row_share, row_share, 2)
    fast_rows = fast_apply(chosen, queries).reshape(row_count, heads_here * feature_count)
    partial_out = jnp.dot(fast_rows, w_out, preferred_element_type=jnp.float32)
    fast_sum = lax.psum_scatter(
        partial_out.astype(jnp.bfloat16), "head", scatter_dimension=1, tiled=True
    ).astype(jnp.float32)
    att_heads = att_q.shape[1] // AD
    queries_att = att_q.reshape(row_count, att_heads, AD)
    keys_att = att_k.reshape(row_count, att_heads, AD)
    values_att = att_v.reshape(row_count, att_heads, AD)
    prior = passed_along((keys_att, values_att), "seq", 1)
    keys_all = jnp.concatenate([prior[0], keys_att], axis=0)
    values_all = jnp.concatenate([prior[1], values_att], axis=0)
    attended = attend(queries_att, keys_all, values_all, position * row_count, row_count)
    attended = attended.reshape(row_count, att_heads * AD)
    return ((attended + fast_sum).astype(jnp.bfloat16), final_weights)


def dot_on(left, right, left_dim, right_dim):
    return lax.dot_general(
        left, right, (((left_dim,), (right_dim,)), ((), ())), preferred_element_type=jnp.float32
    )


def gradient_body(k_ref, v_ref, r_ref, wg_ref, wu_ref, wd_ref, g_ref):
    keys_in = k_ref[...]
    gate_pre = dot_on(keys_in, wg_ref[0], 1, 0)
    up_pre = dot_on(keys_in, wu_ref[0], 1, 0)
    weighted = (r_ref[0] * v_ref[...].astype(jnp.float32)).astype(jnp.bfloat16)
    back = -dot_on(weighted, wd_ref[0], 1, 1)
    sigmoid_val = 1.0 / (1.0 + jnp.exp(-gate_pre))
    silu_val = gate_pre * sigmoid_val
    activated = (silu_val * up_pre).astype(jnp.bfloat16)
    up_in = (back * silu_val).astype(jnp.bfloat16)
    slope = sigmoid_val * (1.0 + gate_pre * (1.0 - sigmoid_val))
    gate_in = (back * up_pre * slope).astype(jnp.bfloat16)
    g_ref[0, 0] = dot_on(keys_in, gate_in, 0, 0).astype(jnp.bfloat16)
    g_ref[1, 0] = dot_on(keys_in, up_in, 0, 0).astype(jnp.bfloat16)
    g_ref[2, 0] = -dot_on(activated, weighted, 0, 0).astype(jnp.bfloat16)


def gradient_call(weights, keys_in, values_in, rate_cols):
    heads, feature, _ = weights[0].shape
    rows = keys_in.shape[0]
    rows_spec = pl.BlockSpec((rows, feature), lambda h: (0, h))
    weight_spec = pl.BlockSpec((1, feature, feature), lambda h: (h, 0, 0))
    return pl.pallas_call(
        gradient_body,
        grid=(heads,),
        in_specs=[rows_spec, rows_spec, pl.BlockSpec((1, rows, 1), lambda h: (h, 0, 0))]
        + [weight_spec] * KINDS,
        out_specs=pl.BlockSpec((KINDS, 1, feature, feature), lambda h: (0, h, 0, 0)),
        out_shape=jax.ShapeDtypeStruct((KINDS, heads, feature, feature), jnp.bfloat16),
        compiler_params=pltpu.CompilerParams(vmem_limit_bytes=VMEM_LIMIT),
        name="gradients",
    )(keys_in, values_in, rate_cols, *weights)


def apply_body(q_ref, wg_ref, wu_ref, wd_ref, o_ref):
    queries = q_ref[...]
    gate_pre = dot_on(queries, wg_ref[0], 1, 0)
    up_pre = dot_on(queries, wu_ref[0], 1, 0)
    activated = (gate_pre / (1.0 + jnp.exp(-gate_pre)) * up_pre).astype(jnp.bfloat16)
    output = dot_on(activated, wd_ref[0], 1, 0)
    factor = lax.rsqrt(jnp.mean(output * output, axis=-1, keepdims=True) + 1e-06)
    o_ref[...] = (output * factor).astype(jnp.bfloat16)


def apply_call(weights, queries):
    heads, feature, _ = weights[0].shape
    rows = queries.shape[0]
    rows_spec = pl.BlockSpec((rows, feature), lambda h: (0, h))
    weight_spec = pl.BlockSpec((1, feature, feature), lambda h: (h, 0, 0))
    return pl.pallas_call(
        apply_body,
        grid=(heads,),
        in_specs=[rows_spec] + [weight_spec] * KINDS,
        out_specs=rows_spec,
        out_shape=jax.ShapeDtypeStruct(queries.shape, jnp.bfloat16),
        compiler_params=pltpu.CompilerParams(vmem_limit_bytes=VMEM_LIMIT),
        name="fast_apply",
    )(queries, *weights)


def attention_body(q_ref, kp_ref, vp_ref, k_ref, v_ref, o_ref):
    rows = q_ref.shape[0]
    first = lax.axis_index("seq") == 0
    row = lax.broadcasted_iota(jnp.int32, (rows, rows), 0)
    col = lax.broadcasted_iota(jnp.int32, (rows, rows), 1)
    column_floor = jnp.where(first, rows, 0)
    prior_ok = (col > row) & (col >= column_floor)
    own_ok = col <= row
    for head in range(q_ref.shape[1] // AD):
        lanes = slice(head * AD, (head + 1) * AD)
        queries = q_ref[:, lanes]
        prior = dot_on(queries, kp_ref[:, lanes], 1, 1) * AD ** (-0.5)
        own = dot_on(queries, k_ref[:, lanes], 1, 1) * AD ** (-0.5)
        prior = jnp.where(prior_ok, prior, -1e30)
        own = jnp.where(own_ok, own, -1e30)
        top = jnp.max(jnp.maximum(prior, own), axis=-1, keepdims=True)
        prior = jnp.exp(prior - top)
        own = jnp.exp(own - top)
        scale = 1.0 / jnp.sum(prior + own, axis=-1, keepdims=True)
        prior = (prior * scale).astype(jnp.bfloat16)
        own = (own * scale).astype(jnp.bfloat16)
        o_ref[:, lanes] = (
            dot_on(prior, vp_ref[:, lanes], 1, 0) + dot_on(own, v_ref[:, lanes], 1, 0)
        ).astype(o_ref.dtype)


def attention_call(queries, prior_keys, prior_values, keys_in, values_in):
    rows, width = queries.shape
    heads = width // AD
    group = 2 * AD if heads % 2 == 0 else AD
    spec = pl.BlockSpec((rows, group), lambda h: (0, h))
    return pl.pallas_call(
        attention_body,
        grid=(width // group,),
        in_specs=[spec] * 5,
        out_specs=spec,
        out_shape=jax.ShapeDtypeStruct(queries.shape, jnp.float32),
        compiler_params=pltpu.CompilerParams(vmem_limit_bytes=VMEM_LIMIT),
        name="attention",
    )(queries, prior_keys, prior_values, keys_in, values_in)


def newton_step(y_ref, kind):
    first, second, third = NEWTON_COEFFS
    matrix = y_ref[kind]
    gram = dot_on(matrix, matrix, 1, 1).astype(jnp.bfloat16)
    square = dot_on(gram, gram, 1, 0)
    poly = (second * gram.astype(jnp.float32) + third * square).astype(jnp.bfloat16)
    y_ref[kind] = (first * matrix.astype(jnp.float32) + dot_on(poly, matrix, 1, 0)).astype(
        jnp.bfloat16
    )


def update_body(span, seq_count, g_ref, wg_ref, wu_ref, wd_ref, *refs):
    last = span == SPANS - 1
    outs = refs[: 1 if last else KINDS]
    (near, total, far, x_ref, y_ref, new_ref) = refs[len(outs) : len(outs) + 6]
    (send_near, recv_near, send_far, recv_far, pair_sem, send_out, recv_out, ready) = refs[
        len(outs) + 6 :
    ]
    w_refs = (wg_ref, wu_ref, wd_ref)
    per_span = seq_count // SPANS
    chips = per_span // 2
    feature = g_ref.shape[-1]
    half = feature // 2
    me = lax.axis_index("seq")
    my_span = me // per_span
    place = me % per_span
    chip = place // 2
    core = place % 2
    mate = me + 1 - 2 * core
    column = chip % 2
    layer = chip // 2
    own_rows = pl.ds(pl.multiple_of(core * half, half), half)
    mate_rows = pl.ds(pl.multiple_of((1 - core) * half, half), half)
    in_span = my_span == span

    def remote(src, dst, send, recv, device):
        return pltpu.make_async_remote_copy(
            src_ref=src, dst_ref=dst, send_sem=send, recv_sem=recv,
            device_id={"seq": device}, device_id_type=MESH,
        )

    def at_place(which_span, which_chip):
        return which_span * per_span + 2 * which_chip + core

    barrier = pltpu.get_barrier_semaphore()
    if last:
        for step in range(1, seq_count):
            pl.semaphore_signal(
                barrier, inc=1, device_id={"seq": (me + step) % seq_count}, device_id_type=MESH
            )
        pl.semaphore_wait(barrier, seq_count - 1)
    else:
        for step in range(1, per_span):
            peer = my_span * per_span + (place + step) % per_span
            pl.semaphore_signal(barrier, inc=1, device_id={"seq": peer}, device_id_type=MESH)

        @pl.when(in_span)
        def _():
            pl.semaphore_signal(
                barrier, inc=1, device_id={"seq": at_place(span + 1, column)}, device_id_type=MESH
            )

        @pl.when(in_span)
        def _():
            pl.semaphore_wait(barrier, per_span - 1)

        @pl.when(jnp.logical_not(in_span) & (layer == 0))
        def _():
            pl.semaphore_wait(barrier, per_span - 1 + 2)

        @pl.when(jnp.logical_not(in_span) & (layer != 0))
        def _():
            pl.semaphore_wait(barrier, per_span - 1)

    @pl.when(in_span)
    def _():
        targets = [(chip + step) % chips for step in range(1, chips)] + [chip]
        near_copies = []
        for slot, target in enumerate(targets):
            copy = remote(
                g_ref.at[:, target, mate_rows], near.at[:, slot],
                send_near.at[slot], recv_near.at[slot], mate,
            )
            copy.start()
            near_copies.append(copy)
        far_copies = []
        for slot, target in enumerate(targets[:-1]):
            near_copies[slot].wait_recv()
            for kind in range(KINDS):
                total[kind, slot] = (
                    g_ref[kind, target, own_rows].astype(jnp.float32)
                    + near[kind, slot].astype(jnp.float32)
                ).astype(jnp.bfloat16)
            copy = remote(
                total.at[:, slot], far.at[:, slot], send_far.at[slot], recv_far.at[slot],
                at_place(span, target),
            )
            copy.start()
            far_copies.append(copy)
        if not last:
            for kind in range(KINDS):
                outs[kind][...] = w_refs[kind][...]
        near_copies[-1].wait_recv()
        for copy in far_copies:
            copy.wait_recv()
        for kind in range(KINDS):
            summed = g_ref[kind, chip, own_rows].astype(jnp.float32)
            summed = summed + near[kind, chips - 1].astype(jnp.float32)
            for slot in range(chips - 1):
                summed = summed + far[kind, slot].astype(jnp.float32)
            x_ref[kind, own_rows] = summed.astype(jnp.bfloat16)
        pair = remote(
            x_ref.at[:, own_rows], x_ref.at[:, own_rows], pair_sem.at[0], pair_sem.at[1], mate
        )
        pair.start()
        for copy in near_copies:
            copy.wait_send()
        for copy in far_copies:
            copy.wait_send()
        pair.wait()
        if not last:
            pl.semaphore_wait(ready, 1)
        out_copies = []
        for kind in range(KINDS):
            gathered = x_ref[kind].astype(jnp.float32)
            norm = jnp.sqrt(jnp.sum(gathered * gathered, keepdims=True) + 1e-06)
            y_ref[kind] = (gathered / norm).astype(jnp.bfloat16)

            @pl.loop(0, NS_STEPS)
            def _(step):
                newton_step(y_ref, kind)

            unmoved = w_refs[kind][chip].astype(jnp.float32)
            moved = unmoved - y_ref[kind].astype(jnp.float32)
            target = jnp.sqrt(jnp.sum(unmoved * unmoved, axis=0, keepdims=True) + 1e-06)
            current = jnp.sqrt(jnp.sum(moved * moved, axis=0, keepdims=True) + 1e-06)
            new_ref[kind] = (moved * (target / current)).astype(jnp.bfloat16)
            if not last:
                copy = remote(
                    new_ref.at[kind, own_rows], outs[kind].at[chip, own_rows],
                    send_out.at[0, kind, 0], recv_out.at[core, kind, chip],
                    at_place(span + 1, column),
                )
                copy.start()
                out_copies.append(copy)
        if last:
            share = feature // seq_count
            chip_count = seq_count // 2
            here = pl.ds(pl.multiple_of(me * share, share), share)
            for step in range(1, chip_count):
                device = 2 * ((me // 2 + step) % chip_count) + core
                there = pl.ds(pl.multiple_of(device * share, share), share)
                copy = remote(
                    new_ref.at[:, there], outs[0].at[:, chip],
                    send_out.at[step], recv_out.at[chip], device,
                )
                copy.start()
                out_copies.append(copy)
            for kind in range(KINDS):
                outs[0][kind, chip] = new_ref[kind, here]
        for copy in out_copies:
            copy.wait_send()

    if last:
        for owner in range(chips):
            @pl.when(jnp.logical_not(in_span & (chip == owner)))
            def _():
                remote(
                    new_ref.at[:, pl.ds(0, feature // seq_count)], outs[0].at[:, owner],
                    send_out.at[0], recv_out.at[owner], mate,
                ).wait_recv()
        return

    @pl.when(jnp.logical_not(in_span))
    def _():
        @pl.when(layer == 0)
        def _():
            for owner_layer in range(2):
                pl.semaphore_signal(
                    ready, inc=1, device_id={"seq": at_place(span, 2 * owner_layer + column)},
                    device_id_type=MESH,
                )

        def passing(kind, owner, lane, device):
            block = outs[kind].at[owner, own_rows]
            return remote(
                block, block, send_out.at[lane, kind, owner], recv_out.at[core, kind, owner], device
            )

        chunks = [(kind, owner_layer) for kind in range(KINDS) for owner_layer in (1, 0)]
        across = at_place(my_span, 2 * layer + 1 - column)
        beyond = at_place(my_span, 2 + column)

        def cross_chunk(kind, owner_layer):
            to_mate = passing(kind, 2 * owner_layer + 1 - column, 0, mate)
            to_mate.wait_recv()
            to_mate.start()

        for number, (kind, owner_layer) in enumerate(chunks):
            owner = 2 * owner_layer + column
            passing(kind, owner, 0, mate).wait_recv()

            @pl.when(layer == 0)
            def _():
                passing(kind, owner, 2, beyond).start()

            passing(kind, owner, 1, across).start()
            passing(kind, owner, 0, mate).start()
            if number:
                cross_chunk(*chunks[number - 1])
        cross_chunk(*chunks[-1])
        for kind, owner_layer in chunks:
            for owner in (2 * owner_layer + column, 2 * owner_layer + 1 - column):
                other = outs[kind].at[owner, mate_rows]
                remote(
                    other, other, send_out.at[0, kind, owner],
                    recv_out.at[1 - core, kind, owner], mate,
                ).wait_recv()
                passing(kind, owner, 0, mate).wait_send()
            owner = 2 * owner_layer + column
            passing(kind, owner, 1, across).wait_send()

            @pl.when(layer == 0)
            def _():
                passing(kind, owner, 2, beyond).wait_send()


def update_call(span, seq_count, grads, weights):
    last = span == SPANS - 1
    _, heads, feature, _ = grads.shape
    chips = seq_count // SPANS // 2
    half = feature // 2
    vmem = pl.BlockSpec(memory_space=pltpu.VMEM)
    if last:
        out_shape = [
            jax.ShapeDtypeStruct((KINDS, heads, feature // seq_count, feature), jnp.bfloat16)
        ]
        out_sems = [
            pltpu.SemaphoreType.DMA((seq_count // 2,)),
            pltpu.SemaphoreType.DMA((chips,)),
        ]
    else:
        out_shape = [jax.ShapeDtypeStruct(weights[0].shape, jnp.bfloat16)] * KINDS
        out_sems = [
            pltpu.SemaphoreType.DMA((3, KINDS, heads)),
            pltpu.SemaphoreType.DMA((2, KINDS, heads)),
        ]
    return pl.pallas_call(
        functools.partial(update_body, span, seq_count),
        out_shape=out_shape,
        in_specs=[vmem] * 4,
        out_specs=[vmem] * len(out_shape),
        scratch_shapes=[
            pltpu.VMEM((KINDS, chips, half, feature), jnp.bfloat16),
            pltpu.VMEM((KINDS, chips - 1, half, feature), jnp.bfloat16),
            pltpu.VMEM((KINDS, chips - 1, half, feature), jnp.bfloat16),
            pltpu.VMEM((KINDS, feature, feature), jnp.bfloat16),
            pltpu.VMEM((KINDS, feature, feature), jnp.bfloat16),
            pltpu.VMEM((KINDS, feature, feature), jnp.bfloat16),
            pltpu.SemaphoreType.DMA((chips,)),
            pltpu.SemaphoreType.DMA((chips,)),
            pltpu.SemaphoreType.DMA((chips - 1,)),
            pltpu.SemaphoreType.DMA((chips - 1,)),
            pltpu.SemaphoreType.DMA((2,)),
            *out_sems,
            pltpu.SemaphoreType.REGULAR,
        ],
        compiler_params=pltpu.CompilerParams(
            collective_id=span, has_side_effects=True, vmem_limit_bytes=VMEM_LIMIT
        ),
        cost_estimate=pl.CostEstimate(
            flops=60_000_000_000, bytes_accessed=2**28, transcendentals=0
        ),
        name=f"update{span}",
    )(grads, *weights)


def owned_on_device(
    fast_q, fast_k, fast_v, rates, w_gate, w_up, w_down, w_out, att_q, att_k, att_v
):
    seq_count = lax.axis_size("seq")
    early = lax.axis_index("seq") < seq_count // SPANS
    start = (w_gate, w_up, w_down)
    rate_cols = rates[:, :, None]
    heads, feature, _ = w_gate.shape
    prior_k = passed_along(att_k, "seq", 1)
    prior_v = passed_along(att_v, "seq", 1)

    def attention():
        return attention_call(att_q, prior_k, prior_v, att_k, att_v)

    def slopes(weights):
        return gradient_call(weights, fast_k, fast_v, rate_cols)

    grads = lax.cond(
        early,
        lambda: slopes(start),
        lambda: jnp.zeros((KINDS, heads, feature, feature), jnp.bfloat16),
    )
    waited = lax.cond(early, lambda: jnp.zeros(att_q.shape, jnp.float32), attention)
    grads, waited = lax.optimization_barrier((grads, waited))
    weights = update_call(0, seq_count, grads, start)
    grads, attended = lax.cond(
        early,
        lambda: (grads, attention()),
        lambda: (slopes(weights), waited),
    )
    fast_rows = apply_call(weights, fast_q)
    partial_out = jnp.dot(fast_rows, w_out, preferred_element_type=jnp.float32)
    partial_out = partial_out.astype(jnp.bfloat16)
    grads, partial_out = lax.optimization_barrier((grads, partial_out))
    fast_sum = lax.psum_scatter(partial_out, "head", scatter_dimension=1, tiled=True)
    (final_weights,) = update_call(1, seq_count, grads, weights)
    return ((attended + fast_sum.astype(jnp.float32)).astype(jnp.bfloat16), final_weights)


def solution(mesh):
    in_specs = (
        P("seq", "head"),
        P("seq", "head"),
        P("seq", "head"),
        P("head", "seq"),
        P("head", None, None),
        P("head", None, None),
        P("head", None, None),
        P("head", None),
        P("seq", "head"),
        P("seq", "head"),
        P("seq", "head"),
    )
    out_specs = (P("seq", "head"), P(None, "head", "seq", None))
    owned = mesh.shape["seq"] == 4 * 2 * SPANS

    def either(*arrays):
        held = arrays[4].shape[0] == mesh.shape["seq"] // (2 * SPANS)
        return (owned_on_device if owned and held else on_device)(*arrays)

    return jax.shard_map(
        either, mesh=mesh, in_specs=in_specs, out_specs=out_specs, check_vma=False
    )
```

```python
import functools

import jax
import jax.numpy as jnp
from jax import lax
from jax.experimental import pallas as pl
from jax.experimental.pallas import tpu as pltpu
from jax.sharding import PartitionSpec as P

AD = 128
SPANS = 2
NS_STEPS = 2
MESH = pl.DeviceIdType.MESH
VMEM_LIMIT = 52 * 1024 * 1024
KINDS = 3


NEWTON_COEFFS = (3.4445, -4.775, 2.0315)


def passed_along(block, axis, distance):
    devices = range(lax.axis_size(axis))
    route = [(i - distance, i) for i in devices if i - distance in devices]
    return lax.ppermute(block, axis, route)


def silu_slope(values):
    sigmoid_val = jax.nn.sigmoid(values)
    return sigmoid_val * (1.0 + values * (1.0 - sigmoid_val))


def product(pattern, left_op, right_op):
    return jnp.einsum(pattern, left_op, right_op, preferred_element_type=jnp.float32)


def fast_apply(weights, queries):
    w_first, w_second, w_third = weights
    gate_pre = product("nhi,hij->nhj", queries, w_first)
    up_pre = product("nhi,hij->nhj", queries, w_second)
    activated = (jax.nn.silu(gate_pre) * up_pre).astype(jnp.bfloat16)
    output = product("nhj,hjk->nhk", activated, w_third)
    factor = lax.rsqrt(jnp.mean(output * output, axis=-1, keepdims=True) + 1e-06)
    return (output * factor).astype(jnp.bfloat16)


def gradients(weights, keys_in, values_in, rate_rows):
    w_first, w_second, w_third = weights
    gate_pre = product("nhi,hij->nhj", keys_in, w_first)
    up_pre = product("nhi,hij->nhj", keys_in, w_second)
    activated = (jax.nn.silu(gate_pre) * up_pre).astype(jnp.bfloat16)
    weighted = (rate_rows[:, :, None] * values_in.astype(jnp.float32)).astype(jnp.bfloat16)
    grad_third = -product("nhj,nhk->hjk", activated, weighted)
    back = -product("nhk,hjk->nhj", weighted, w_third)
    up_in = (back * jax.nn.silu(gate_pre)).astype(jnp.bfloat16)
    gate_in = (back * up_pre * silu_slope(gate_pre)).astype(jnp.bfloat16)
    grad_first = product("nhi,nhj->hij", keys_in, gate_in)
    grad_second = product("nhi,nhj->hij", keys_in, up_in)
    return (grad_first, grad_second, grad_third)


def scale_down(summed):
    squares = jnp.sum(summed * summed, axis=(1, 2))
    return (summed / jnp.sqrt(squares + 1e-06)[:, None, None]).astype(jnp.bfloat16)


def newton_schulz(matrix):
    first, second, third = NEWTON_COEFFS
    for iteration in range(NS_STEPS):
        gram = product("mij,mkj->mik", matrix, matrix).astype(jnp.bfloat16)
        square = product("mij,mjk->mik", gram, gram)
        poly = (second * gram.astype(jnp.float32) + third * square).astype(jnp.bfloat16)
        matrix = (
            first * matrix.astype(jnp.float32) + product("mij,mjk->mik", poly, matrix)
        ).astype(jnp.bfloat16)
    return matrix


def renorm(weight, ortho):
    unmoved = weight.astype(jnp.float32)
    moved = unmoved - ortho.astype(jnp.float32)
    target = jnp.sqrt(jnp.sum(unmoved * unmoved, axis=1, keepdims=True) + 1e-06)
    current = jnp.sqrt(jnp.sum(moved * moved, axis=1, keepdims=True) + 1e-06)
    return (moved * (target / current)).astype(jnp.bfloat16)


def attend(queries, keys_all, values_all, offset, window):
    block = queries.shape[0]
    scores = product("qhd,khd->hqk", queries, keys_all) * queries.shape[-1] ** (-0.5)
    query_pos = offset + lax.broadcasted_iota(jnp.int32, (block, 2 * block), 0)
    key_pos = offset - block + lax.broadcasted_iota(jnp.int32, (block, 2 * block), 1)
    allowed = (key_pos <= query_pos) & (key_pos > query_pos - window) & (key_pos >= 0)
    scores = jnp.where(allowed[None], scores, -1e30)
    row_max = jnp.max(scores, axis=-1, keepdims=True)
    exp_scores = jnp.exp(scores - row_max)
    probs = (exp_scores / jnp.sum(exp_scores, axis=-1, keepdims=True)).astype(jnp.bfloat16)
    return product("hqk,khd->qhd", probs, values_all)


def on_device(fast_q, fast_k, fast_v, rates, w_gate, w_up, w_down, w_out, att_q, att_k, att_v):
    row_count = fast_q.shape[0]
    heads_here = w_gate.shape[0]
    feature_count = w_gate.shape[1]
    queries = fast_q.reshape(row_count, heads_here, feature_count)
    keys_fast = fast_k.reshape(row_count, heads_here, feature_count)
    values_fast = fast_v.reshape(row_count, heads_here, feature_count)
    rate_rows = rates.T
    seq_count = lax.axis_size("seq")
    position = lax.axis_index("seq")
    group_id = position // (seq_count // SPANS)
    weights = (w_gate, w_up, w_down)
    chosen = weights
    for span in range(SPANS):
        grads = gradients(weights, keys_fast, values_fast, rate_rows)
        stacked = jnp.concatenate(grads, axis=0)
        stacked = jnp.where(group_id == span, stacked, jnp.zeros_like(stacked))
        summed = lax.psum(stacked.astype(jnp.bfloat16), "seq").astype(jnp.float32)
        start_matrix = scale_down(summed)
        ortho = newton_schulz(start_matrix)
        pieces = ortho.reshape(3, heads_here, feature_count, feature_count)
        weights = tuple((renorm(weights[member], pieces[member]) for member in range(3)))
        if span + 1 < SPANS:
            chosen = tuple(
                (
                    jnp.where(group_id == span + 1, fresh, older)
                    for fresh, older in zip(weights, chosen)
                )
            )
    row_share = feature_count // seq_count
    final_all = jnp.stack(weights, axis=0)
    final_weights = lax.dynamic_slice_in_dim(final_all, position * row_share, row_share, 2)
    fast_rows = fast_apply(chosen, queries).reshape(row_count, heads_here * feature_count)
    partial_out = jnp.dot(fast_rows, w_out, preferred_element_type=jnp.float32)
    fast_sum = lax.psum_scatter(
        partial_out.astype(jnp.bfloat16), "head", scatter_dimension=1, tiled=True
    ).astype(jnp.float32)
    att_heads = att_q.shape[1] // AD
    queries_att = att_q.reshape(row_count, att_heads, AD)
    keys_att = att_k.reshape(row_count, att_heads, AD)
    values_att = att_v.reshape(row_count, att_heads, AD)
    prior = passed_along((keys_att, values_att), "seq", 1)
    keys_all = jnp.concatenate([prior[0], keys_att], axis=0)
    values_all = jnp.concatenate([prior[1], values_att], axis=0)
    attended = attend(queries_att, keys_all, values_all, position * row_count, row_count)
    attended = attended.reshape(row_count, att_heads * AD)
    return ((attended + fast_sum).astype(jnp.bfloat16), final_weights)


def dot_on(left, right, left_dim, right_dim):
    return lax.dot_general(
        left, right, (((left_dim,), (right_dim,)), ((), ())), preferred_element_type=jnp.float32
    )


def gradient_body(k_ref, v_ref, r_ref, wg_ref, wu_ref, wd_ref, g_ref):
    keys_in = k_ref[...]
    gate_pre = dot_on(keys_in, wg_ref[0], 1, 0)
    up_pre = dot_on(keys_in, wu_ref[0], 1, 0)
    weighted = (r_ref[0] * v_ref[...].astype(jnp.float32)).astype(jnp.bfloat16)
    back = -dot_on(weighted, wd_ref[0], 1, 1)
    sigmoid_val = 1.0 / (1.0 + jnp.exp(-gate_pre))
    silu_val = gate_pre * sigmoid_val
    activated = (silu_val * up_pre).astype(jnp.bfloat16)
    up_in = (back * silu_val).astype(jnp.bfloat16)
    slope = sigmoid_val * (1.0 + gate_pre * (1.0 - sigmoid_val))
    gate_in = (back * up_pre * slope).astype(jnp.bfloat16)
    g_ref[0, 0] = dot_on(keys_in, gate_in, 0, 0).astype(jnp.bfloat16)
    g_ref[1, 0] = dot_on(keys_in, up_in, 0, 0).astype(jnp.bfloat16)
    g_ref[2, 0] = -dot_on(activated, weighted, 0, 0).astype(jnp.bfloat16)


def gradient_call(weights, keys_in, values_in, rate_cols):
    heads, feature, _ = weights[0].shape
    rows = keys_in.shape[0]
    rows_spec = pl.BlockSpec((rows, feature), lambda h: (0, h))
    weight_spec = pl.BlockSpec((1, feature, feature), lambda h: (h, 0, 0))
    return pl.pallas_call(
        gradient_body,
        grid=(heads,),
        in_specs=[rows_spec, rows_spec, pl.BlockSpec((1, rows, 1), lambda h: (h, 0, 0))]
        + [weight_spec] * KINDS,
        out_specs=pl.BlockSpec((KINDS, 1, feature, feature), lambda h: (0, h, 0, 0)),
        out_shape=jax.ShapeDtypeStruct((KINDS, heads, feature, feature), jnp.bfloat16),
        compiler_params=pltpu.CompilerParams(vmem_limit_bytes=VMEM_LIMIT),
        name="gradients",
    )(keys_in, values_in, rate_cols, *weights)


def apply_body(q_ref, wg_ref, wu_ref, wd_ref, o_ref):
    queries = q_ref[...]
    gate_pre = dot_on(queries, wg_ref[0], 1, 0)
    up_pre = dot_on(queries, wu_ref[0], 1, 0)
    activated = (gate_pre / (1.0 + jnp.exp(-gate_pre)) * up_pre).astype(jnp.bfloat16)
    output = dot_on(activated, wd_ref[0], 1, 0)
    factor = lax.rsqrt(jnp.mean(output * output, axis=-1, keepdims=True) + 1e-06)
    o_ref[...] = (output * factor).astype(jnp.bfloat16)


def apply_call(weights, queries):
    heads, feature, _ = weights[0].shape
    rows = queries.shape[0]
    rows_spec = pl.BlockSpec((rows, feature), lambda h: (0, h))
    weight_spec = pl.BlockSpec((1, feature, feature), lambda h: (h, 0, 0))
    return pl.pallas_call(
        apply_body,
        grid=(heads,),
        in_specs=[rows_spec] + [weight_spec] * KINDS,
        out_specs=rows_spec,
        out_shape=jax.ShapeDtypeStruct(queries.shape, jnp.bfloat16),
        compiler_params=pltpu.CompilerParams(vmem_limit_bytes=VMEM_LIMIT),
        name="fast_apply",
    )(queries, *weights)


def attention_body(q_ref, kp_ref, vp_ref, k_ref, v_ref, o_ref):
    rows = q_ref.shape[0]
    first = lax.axis_index("seq") == 0
    row = lax.broadcasted_iota(jnp.int32, (rows, rows), 0)
    col = lax.broadcasted_iota(jnp.int32, (rows, rows), 1)
    column_floor = jnp.where(first, rows, 0)
    prior_ok = (col > row) & (col >= column_floor)
    own_ok = col <= row
    for head in range(q_ref.shape[1] // AD):
        lanes = slice(head * AD, (head + 1) * AD)
        queries = q_ref[:, lanes]
        prior = dot_on(queries, kp_ref[:, lanes], 1, 1) * AD ** (-0.5)
        own = dot_on(queries, k_ref[:, lanes], 1, 1) * AD ** (-0.5)
        prior = jnp.where(prior_ok, prior, -1e30)
        own = jnp.where(own_ok, own, -1e30)
        top = jnp.max(jnp.maximum(prior, own), axis=-1, keepdims=True)
        prior = jnp.exp(prior - top)
        own = jnp.exp(own - top)
        scale = 1.0 / jnp.sum(prior + own, axis=-1, keepdims=True)
        prior = (prior * scale).astype(jnp.bfloat16)
        own = (own * scale).astype(jnp.bfloat16)
        o_ref[:, lanes] = (
            dot_on(prior, vp_ref[:, lanes], 1, 0) + dot_on(own, v_ref[:, lanes], 1, 0)
        ).astype(o_ref.dtype)


def attention_call(queries, prior_keys, prior_values, keys_in, values_in):
    rows, width = queries.shape
    heads = width // AD
    group = 2 * AD if heads % 2 == 0 else AD
    spec = pl.BlockSpec((rows, group), lambda h: (0, h))
    return pl.pallas_call(
        attention_body,
        grid=(width // group,),
        in_specs=[spec] * 5,
        out_specs=spec,
        out_shape=jax.ShapeDtypeStruct(queries.shape, jnp.float32),
        compiler_params=pltpu.CompilerParams(vmem_limit_bytes=VMEM_LIMIT),
        name="attention",
    )(queries, prior_keys, prior_values, keys_in, values_in)


def newton_step(y_ref, kind):
    first, second, third = NEWTON_COEFFS
    matrix = y_ref[kind]
    gram = dot_on(matrix, matrix, 1, 1).astype(jnp.bfloat16)
    square = dot_on(gram, gram, 1, 0)
    poly = (second * gram.astype(jnp.float32) + third * square).astype(jnp.bfloat16)
    y_ref[kind] = (first * matrix.astype(jnp.float32) + dot_on(poly, matrix, 1, 0)).astype(
        jnp.bfloat16
    )


def update_body(span, seq_count, g_ref, wg_ref, wu_ref, wd_ref, *refs):
    last = span == SPANS - 1
    outs = refs[: 1 if last else KINDS]
    (near, total, far, x_ref, y_ref, new_ref) = refs[len(outs) : len(outs) + 6]
    (send_near, recv_near, send_far, recv_far, pair_sem, send_out, recv_out, ready) = refs[
        len(outs) + 6 :
    ]
    w_refs = (wg_ref, wu_ref, wd_ref)
    per_span = seq_count // SPANS
    chips = per_span // 2
    feature = g_ref.shape[-1]
    half = feature // 2
    me = lax.axis_index("seq")
    my_span = me // per_span
    place = me % per_span
    chip = place // 2
    core = place % 2
    mate = me + 1 - 2 * core
    column = chip % 2
    layer = chip // 2
    own_rows = pl.ds(pl.multiple_of(core * half, half), half)
    mate_rows = pl.ds(pl.multiple_of((1 - core) * half, half), half)
    in_span = my_span == span

    def remote(src, dst, send, recv, device):
        return pltpu.make_async_remote_copy(
            src_ref=src, dst_ref=dst, send_sem=send, recv_sem=recv,
            device_id={"seq": device}, device_id_type=MESH,
        )

    def at_place(which_span, which_chip):
        return which_span * per_span + 2 * which_chip + core

    barrier = pltpu.get_barrier_semaphore()
    if last:
        for step in range(1, seq_count):
            pl.semaphore_signal(
                barrier, inc=1, device_id={"seq": (me + step) % seq_count}, device_id_type=MESH
            )
        pl.semaphore_wait(barrier, seq_count - 1)
    else:
        for step in range(1, per_span):
            peer = my_span * per_span + (place + step) % per_span
            pl.semaphore_signal(barrier, inc=1, device_id={"seq": peer}, device_id_type=MESH)

        @pl.when(in_span)
        def _():
            pl.semaphore_signal(
                barrier, inc=1, device_id={"seq": at_place(span + 1, column)}, device_id_type=MESH
            )

        @pl.when(in_span)
        def _():
            pl.semaphore_wait(barrier, per_span - 1)

        @pl.when(jnp.logical_not(in_span) & (layer == 0))
        def _():
            pl.semaphore_wait(barrier, per_span - 1 + 2)

        @pl.when(jnp.logical_not(in_span) & (layer != 0))
        def _():
            pl.semaphore_wait(barrier, per_span - 1)

    @pl.when(in_span)
    def _():
        targets = [(chip + step) % chips for step in range(1, chips)] + [chip]

        def near_copy(kind, slot):
            return remote(
                g_ref.at[kind, targets[slot], mate_rows], near.at[kind, slot],
                send_near.at[kind, slot], recv_near.at[kind, slot], mate,
            )

        def far_copy(kind, slot):
            return remote(
                total.at[kind, slot], far.at[kind, slot],
                send_far.at[kind, slot], recv_far.at[kind, slot], at_place(span, targets[slot]),
            )

        def pair_copy(kind):
            return remote(
                x_ref.at[kind, own_rows], x_ref.at[kind, own_rows],
                pair_sem.at[0, kind], pair_sem.at[1, kind], mate,
            )

        for kind in range(KINDS):
            for slot in range(chips):
                near_copy(kind, slot).start()
        for kind in range(KINDS):
            for slot, target in enumerate(targets[:-1]):
                near_copy(kind, slot).wait_recv()
                total[kind, slot] = (
                    g_ref[kind, target, own_rows].astype(jnp.float32)
                    + near[kind, slot].astype(jnp.float32)
                ).astype(jnp.bfloat16)
                far_copy(kind, slot).start()
            near_copy(kind, chips - 1).wait_recv()
        if not last:
            for kind in range(KINDS):
                outs[kind][...] = w_refs[kind][...]
        out_copies = []
        for kind in range(KINDS):
            summed = g_ref[kind, chip, own_rows].astype(jnp.float32)
            summed = summed + near[kind, chips - 1].astype(jnp.float32)
            for slot in range(chips - 1):
                far_copy(kind, slot).wait_recv()
                summed = summed + far[kind, slot].astype(jnp.float32)
            x_ref[kind, own_rows] = summed.astype(jnp.bfloat16)
            pair_copy(kind).start()
            pair_copy(kind).wait()
            gathered = x_ref[kind].astype(jnp.float32)
            norm = jnp.sqrt(jnp.sum(gathered * gathered, keepdims=True) + 1e-06)
            y_ref[kind] = (gathered / norm).astype(jnp.bfloat16)

            @pl.loop(0, NS_STEPS)
            def _(step):
                newton_step(y_ref, kind)

            unmoved = w_refs[kind][chip].astype(jnp.float32)
            moved = unmoved - y_ref[kind].astype(jnp.float32)
            target = jnp.sqrt(jnp.sum(unmoved * unmoved, axis=0, keepdims=True) + 1e-06)
            current = jnp.sqrt(jnp.sum(moved * moved, axis=0, keepdims=True) + 1e-06)
            new_ref[kind] = (moved * (target / current)).astype(jnp.bfloat16)
            if not last:
                if kind == 0:
                    pl.semaphore_wait(ready, 1)
                copy = remote(
                    new_ref.at[kind, own_rows], outs[kind].at[chip, own_rows],
                    send_out.at[0, kind, 0], recv_out.at[core, kind, chip],
                    at_place(span + 1, column),
                )
                copy.start()
                out_copies.append(copy)
                continue
            share = feature // seq_count
            chip_count = seq_count // 2
            for step in range(1, chip_count):
                device = 2 * ((me // 2 + step) % chip_count) + core
                there = pl.ds(pl.multiple_of(device * share, share), share)
                copy = remote(
                    new_ref.at[kind, there], outs[0].at[kind, chip],
                    send_out.at[kind, step], recv_out.at[kind, chip], device,
                )
                copy.start()
                out_copies.append(copy)
            here = pl.ds(pl.multiple_of(me * share, share), share)
            outs[0][kind, chip] = new_ref[kind, here]
        for copy in out_copies:
            copy.wait_send()
        for kind in range(KINDS):
            for slot in range(chips):
                near_copy(kind, slot).wait_send()
            for slot in range(chips - 1):
                far_copy(kind, slot).wait_send()

    if last:
        for owner in range(chips):
            @pl.when(jnp.logical_not(in_span & (chip == owner)))
            def _():
                for kind in range(KINDS):
                    remote(
                        new_ref.at[kind, pl.ds(0, feature // seq_count)],
                        outs[0].at[kind, owner],
                        send_out.at[kind, 0], recv_out.at[kind, owner], mate,
                    ).wait_recv()
        return

    @pl.when(jnp.logical_not(in_span))
    def _():
        @pl.when(layer == 0)
        def _():
            for owner_layer in range(2):
                pl.semaphore_signal(
                    ready, inc=1, device_id={"seq": at_place(span, 2 * owner_layer + column)},
                    device_id_type=MESH,
                )

        def passing(kind, owner, lane, device):
            block = outs[kind].at[owner, own_rows]
            return remote(
                block, block, send_out.at[lane, kind, owner], recv_out.at[core, kind, owner], device
            )

        chunks = [(kind, owner_layer) for kind in range(KINDS) for owner_layer in (1, 0)]
        across = at_place(my_span, 2 * layer + 1 - column)
        beyond = at_place(my_span, 2 + column)

        def cross_chunk(kind, owner_layer):
            to_mate = passing(kind, 2 * owner_layer + 1 - column, 0, mate)
            to_mate.wait_recv()
            to_mate.start()

        for number, (kind, owner_layer) in enumerate(chunks):
            owner = 2 * owner_layer + column
            passing(kind, owner, 0, mate).wait_recv()

            @pl.when(layer == 0)
            def _():
                passing(kind, owner, 2, beyond).start()

            passing(kind, owner, 1, across).start()
            passing(kind, owner, 0, mate).start()
            if number:
                cross_chunk(*chunks[number - 1])
        cross_chunk(*chunks[-1])
        for kind, owner_layer in chunks:
            for owner in (2 * owner_layer + column, 2 * owner_layer + 1 - column):
                other = outs[kind].at[owner, mate_rows]
                remote(
                    other, other, send_out.at[0, kind, owner],
                    recv_out.at[1 - core, kind, owner], mate,
                ).wait_recv()
                passing(kind, owner, 0, mate).wait_send()
            owner = 2 * owner_layer + column
            passing(kind, owner, 1, across).wait_send()

            @pl.when(layer == 0)
            def _():
                passing(kind, owner, 2, beyond).wait_send()


def update_call(span, seq_count, grads, weights):
    last = span == SPANS - 1
    _, heads, feature, _ = grads.shape
    chips = seq_count // SPANS // 2
    half = feature // 2
    vmem = pl.BlockSpec(memory_space=pltpu.VMEM)
    if last:
        out_shape = [
            jax.ShapeDtypeStruct((KINDS, heads, feature // seq_count, feature), jnp.bfloat16)
        ]
        out_sems = [
            pltpu.SemaphoreType.DMA((KINDS, seq_count // 2)),
            pltpu.SemaphoreType.DMA((KINDS, chips)),
        ]
    else:
        out_shape = [jax.ShapeDtypeStruct(weights[0].shape, jnp.bfloat16)] * KINDS
        out_sems = [
            pltpu.SemaphoreType.DMA((3, KINDS, heads)),
            pltpu.SemaphoreType.DMA((2, KINDS, heads)),
        ]
    return pl.pallas_call(
        functools.partial(update_body, span, seq_count),
        out_shape=out_shape,
        in_specs=[vmem] * 4,
        out_specs=[vmem] * len(out_shape),
        scratch_shapes=[
            pltpu.VMEM((KINDS, chips, half, feature), jnp.bfloat16),
            pltpu.VMEM((KINDS, chips - 1, half, feature), jnp.bfloat16),
            pltpu.VMEM((KINDS, chips - 1, half, feature), jnp.bfloat16),
            pltpu.VMEM((KINDS, feature, feature), jnp.bfloat16),
            pltpu.VMEM((KINDS, feature, feature), jnp.bfloat16),
            pltpu.VMEM((KINDS, feature, feature), jnp.bfloat16),
            pltpu.SemaphoreType.DMA((KINDS, chips)),
            pltpu.SemaphoreType.DMA((KINDS, chips)),
            pltpu.SemaphoreType.DMA((KINDS, chips - 1)),
            pltpu.SemaphoreType.DMA((KINDS, chips - 1)),
            pltpu.SemaphoreType.DMA((2, KINDS)),
            *out_sems,
            pltpu.SemaphoreType.REGULAR,
        ],
        compiler_params=pltpu.CompilerParams(
            collective_id=span, has_side_effects=True, vmem_limit_bytes=VMEM_LIMIT
        ),
        cost_estimate=pl.CostEstimate(
            flops=60_000_000_000, bytes_accessed=2**28, transcendentals=0
        ),
        name=f"update{span}",
    )(grads, *weights)


def owned_on_device(
    fast_q, fast_k, fast_v, rates, w_gate, w_up, w_down, w_out, att_q, att_k, att_v
):
    seq_count = lax.axis_size("seq")
    early = lax.axis_index("seq") < seq_count // SPANS
    start = (w_gate, w_up, w_down)
    rate_cols = rates[:, :, None]
    heads, feature, _ = w_gate.shape
    count = seq_count // SPANS

    def prior_of(blocks, low, high):
        route = [(i - 1, i) for i in range(max(low, 1), high)]
        return tuple(lax.ppermute(block, "seq", route) for block in blocks)

    def attention(prior):
        return attention_call(att_q, *prior, att_k, att_v)

    def slopes(weights):
        return gradient_call(weights, fast_k, fast_v, rate_cols)

    grads = lax.cond(
        early,
        lambda: slopes(start),
        lambda: jnp.zeros((KINDS, heads, feature, feature), jnp.bfloat16),
    )
    prior = prior_of((att_k, att_v), count, seq_count)
    waited = lax.cond(
        early, lambda: jnp.zeros(att_q.shape, jnp.float32), lambda: attention(prior)
    )
    grads, waited = lax.optimization_barrier((grads, waited))
    weights = update_call(0, seq_count, grads, start)
    weights, later = lax.optimization_barrier((weights, (att_k, att_v)))
    early_prior = prior_of(later, 0, count)
    grads, attended = lax.cond(
        early,
        lambda: (grads, attention(early_prior)),
        lambda: (slopes(weights), waited),
    )
    fast_rows = apply_call(weights, fast_q)
    partial_out = jnp.dot(fast_rows, w_out, preferred_element_type=jnp.float32)
    partial_out = partial_out.astype(jnp.bfloat16)
    grads, partial_out = lax.optimization_barrier((grads, partial_out))
    fast_sum = lax.psum_scatter(partial_out, "head", scatter_dimension=1, tiled=True)
    (final_weights,) = update_call(1, seq_count, grads, weights)
    return ((attended + fast_sum.astype(jnp.float32)).astype(jnp.bfloat16), final_weights)


def solution(mesh):
    in_specs = (
        P("seq", "head"),
        P("seq", "head"),
        P("seq", "head"),
        P("head", "seq"),
        P("head", None, None),
        P("head", None, None),
        P("head", None, None),
        P("head", None),
        P("seq", "head"),
        P("seq", "head"),
        P("seq", "head"),
    )
    out_specs = (P("seq", "head"), P(None, "head", "seq", None))
    owned = mesh.shape["seq"] == 4 * 2 * SPANS

    def either(*arrays):
        held = arrays[4].shape[0] == mesh.shape["seq"] // (2 * SPANS)
        return (owned_on_device if owned and held else on_device)(*arrays)

    return jax.shard_map(
        either, mesh=mesh, in_specs=in_specs, out_specs=out_specs, check_vma=False
    )
```

```python
import functools

import jax
import jax.numpy as jnp
from jax import lax
from jax.experimental import pallas as pl
from jax.experimental.pallas import tpu as pltpu
from jax.sharding import PartitionSpec as P

AD = 128
SPANS = 2
NS_STEPS = 2
MESH = pl.DeviceIdType.MESH
VMEM_LIMIT = 52 * 1024 * 1024
KINDS = 3


NEWTON_COEFFS = (3.4445, -4.775, 2.0315)


def passed_along(block, axis, distance):
    devices = range(lax.axis_size(axis))
    route = [(i - distance, i) for i in devices if i - distance in devices]
    return lax.ppermute(block, axis, route)


def silu_slope(values):
    sigmoid_val = jax.nn.sigmoid(values)
    return sigmoid_val * (1.0 + values * (1.0 - sigmoid_val))


def product(pattern, left_op, right_op):
    return jnp.einsum(pattern, left_op, right_op, preferred_element_type=jnp.float32)


def fast_apply(weights, queries):
    w_first, w_second, w_third = weights
    gate_pre = product("nhi,hij->nhj", queries, w_first)
    up_pre = product("nhi,hij->nhj", queries, w_second)
    activated = (jax.nn.silu(gate_pre) * up_pre).astype(jnp.bfloat16)
    output = product("nhj,hjk->nhk", activated, w_third)
    factor = lax.rsqrt(jnp.mean(output * output, axis=-1, keepdims=True) + 1e-06)
    return (output * factor).astype(jnp.bfloat16)


def gradients(weights, keys_in, values_in, rate_rows):
    w_first, w_second, w_third = weights
    gate_pre = product("nhi,hij->nhj", keys_in, w_first)
    up_pre = product("nhi,hij->nhj", keys_in, w_second)
    activated = (jax.nn.silu(gate_pre) * up_pre).astype(jnp.bfloat16)
    weighted = (rate_rows[:, :, None] * values_in.astype(jnp.float32)).astype(jnp.bfloat16)
    grad_third = -product("nhj,nhk->hjk", activated, weighted)
    back = -product("nhk,hjk->nhj", weighted, w_third)
    up_in = (back * jax.nn.silu(gate_pre)).astype(jnp.bfloat16)
    gate_in = (back * up_pre * silu_slope(gate_pre)).astype(jnp.bfloat16)
    grad_first = product("nhi,nhj->hij", keys_in, gate_in)
    grad_second = product("nhi,nhj->hij", keys_in, up_in)
    return (grad_first, grad_second, grad_third)


def scale_down(summed):
    squares = jnp.sum(summed * summed, axis=(1, 2))
    return (summed / jnp.sqrt(squares + 1e-06)[:, None, None]).astype(jnp.bfloat16)


def newton_schulz(matrix):
    first, second, third = NEWTON_COEFFS
    for iteration in range(NS_STEPS):
        gram = product("mij,mkj->mik", matrix, matrix).astype(jnp.bfloat16)
        square = product("mij,mjk->mik", gram, gram)
        poly = (second * gram.astype(jnp.float32) + third * square).astype(jnp.bfloat16)
        matrix = (
            first * matrix.astype(jnp.float32) + product("mij,mjk->mik", poly, matrix)
        ).astype(jnp.bfloat16)
    return matrix


def renorm(weight, ortho):
    unmoved = weight.astype(jnp.float32)
    moved = unmoved - ortho.astype(jnp.float32)
    target = jnp.sqrt(jnp.sum(unmoved * unmoved, axis=1, keepdims=True) + 1e-06)
    current = jnp.sqrt(jnp.sum(moved * moved, axis=1, keepdims=True) + 1e-06)
    return (moved * (target / current)).astype(jnp.bfloat16)


def attend(queries, keys_all, values_all, offset, window):
    block = queries.shape[0]
    scores = product("qhd,khd->hqk", queries, keys_all) * queries.shape[-1] ** (-0.5)
    query_pos = offset + lax.broadcasted_iota(jnp.int32, (block, 2 * block), 0)
    key_pos = offset - block + lax.broadcasted_iota(jnp.int32, (block, 2 * block), 1)
    allowed = (key_pos <= query_pos) & (key_pos > query_pos - window) & (key_pos >= 0)
    scores = jnp.where(allowed[None], scores, -1e30)
    row_max = jnp.max(scores, axis=-1, keepdims=True)
    exp_scores = jnp.exp(scores - row_max)
    probs = (exp_scores / jnp.sum(exp_scores, axis=-1, keepdims=True)).astype(jnp.bfloat16)
    return product("hqk,khd->qhd", probs, values_all)


def on_device(fast_q, fast_k, fast_v, rates, w_gate, w_up, w_down, w_out, att_q, att_k, att_v):
    row_count = fast_q.shape[0]
    heads_here = w_gate.shape[0]
    feature_count = w_gate.shape[1]
    queries = fast_q.reshape(row_count, heads_here, feature_count)
    keys_fast = fast_k.reshape(row_count, heads_here, feature_count)
    values_fast = fast_v.reshape(row_count, heads_here, feature_count)
    rate_rows = rates.T
    seq_count = lax.axis_size("seq")
    position = lax.axis_index("seq")
    group_id = position // (seq_count // SPANS)
    weights = (w_gate, w_up, w_down)
    chosen = weights
    for span in range(SPANS):
        grads = gradients(weights, keys_fast, values_fast, rate_rows)
        stacked = jnp.concatenate(grads, axis=0)
        stacked = jnp.where(group_id == span, stacked, jnp.zeros_like(stacked))
        summed = lax.psum(stacked.astype(jnp.bfloat16), "seq").astype(jnp.float32)
        start_matrix = scale_down(summed)
        ortho = newton_schulz(start_matrix)
        pieces = ortho.reshape(3, heads_here, feature_count, feature_count)
        weights = tuple((renorm(weights[member], pieces[member]) for member in range(3)))
        if span + 1 < SPANS:
            chosen = tuple(
                (
                    jnp.where(group_id == span + 1, fresh, older)
                    for fresh, older in zip(weights, chosen)
                )
            )
    row_share = feature_count // seq_count
    final_all = jnp.stack(weights, axis=0)
    final_weights = lax.dynamic_slice_in_dim(final_all, position * row_share, row_share, 2)
    fast_rows = fast_apply(chosen, queries).reshape(row_count, heads_here * feature_count)
    partial_out = jnp.dot(fast_rows, w_out, preferred_element_type=jnp.float32)
    fast_sum = lax.psum_scatter(
        partial_out.astype(jnp.bfloat16), "head", scatter_dimension=1, tiled=True
    ).astype(jnp.float32)
    att_heads = att_q.shape[1] // AD
    queries_att = att_q.reshape(row_count, att_heads, AD)
    keys_att = att_k.reshape(row_count, att_heads, AD)
    values_att = att_v.reshape(row_count, att_heads, AD)
    prior = passed_along((keys_att, values_att), "seq", 1)
    keys_all = jnp.concatenate([prior[0], keys_att], axis=0)
    values_all = jnp.concatenate([prior[1], values_att], axis=0)
    attended = attend(queries_att, keys_all, values_all, position * row_count, row_count)
    attended = attended.reshape(row_count, att_heads * AD)
    return ((attended + fast_sum).astype(jnp.bfloat16), final_weights)


def dot_on(left, right, left_dim, right_dim):
    return lax.dot_general(
        left, right, (((left_dim,), (right_dim,)), ((), ())), preferred_element_type=jnp.float32
    )


def gradient_body(k_ref, v_ref, r_ref, wg_ref, wu_ref, wd_ref, g_ref):
    keys_in = k_ref[...]
    gate_pre = dot_on(keys_in, wg_ref[0], 1, 0)
    up_pre = dot_on(keys_in, wu_ref[0], 1, 0)
    weighted = (r_ref[0] * v_ref[...].astype(jnp.float32)).astype(jnp.bfloat16)
    back = -dot_on(weighted, wd_ref[0], 1, 1)
    sigmoid_val = 1.0 / (1.0 + jnp.exp(-gate_pre))
    silu_val = gate_pre * sigmoid_val
    activated = (silu_val * up_pre).astype(jnp.bfloat16)
    up_in = (back * silu_val).astype(jnp.bfloat16)
    slope = sigmoid_val * (1.0 + gate_pre * (1.0 - sigmoid_val))
    gate_in = (back * up_pre * slope).astype(jnp.bfloat16)
    g_ref[0, 0] = dot_on(keys_in, gate_in, 0, 0).astype(jnp.bfloat16)
    g_ref[1, 0] = dot_on(keys_in, up_in, 0, 0).astype(jnp.bfloat16)
    g_ref[2, 0] = -dot_on(activated, weighted, 0, 0).astype(jnp.bfloat16)


def gradient_call(weights, keys_in, values_in, rate_cols):
    heads, feature, _ = weights[0].shape
    rows = keys_in.shape[0]
    rows_spec = pl.BlockSpec((rows, feature), lambda h: (0, h))
    weight_spec = pl.BlockSpec((1, feature, feature), lambda h: (h, 0, 0))
    return pl.pallas_call(
        gradient_body,
        grid=(heads,),
        in_specs=[rows_spec, rows_spec, pl.BlockSpec((1, rows, 1), lambda h: (h, 0, 0))]
        + [weight_spec] * KINDS,
        out_specs=pl.BlockSpec((KINDS, 1, feature, feature), lambda h: (0, h, 0, 0)),
        out_shape=jax.ShapeDtypeStruct((KINDS, heads, feature, feature), jnp.bfloat16),
        compiler_params=pltpu.CompilerParams(vmem_limit_bytes=VMEM_LIMIT),
        name="gradients",
    )(keys_in, values_in, rate_cols, *weights)


def apply_body(q_ref, wg_ref, wu_ref, wd_ref, o_ref):
    queries = q_ref[...]
    gate_pre = dot_on(queries, wg_ref[0], 1, 0)
    up_pre = dot_on(queries, wu_ref[0], 1, 0)
    activated = (gate_pre / (1.0 + jnp.exp(-gate_pre)) * up_pre).astype(jnp.bfloat16)
    output = dot_on(activated, wd_ref[0], 1, 0)
    factor = lax.rsqrt(jnp.mean(output * output, axis=-1, keepdims=True) + 1e-06)
    o_ref[...] = (output * factor).astype(jnp.bfloat16)


def apply_call(weights, queries):
    heads, feature, _ = weights[0].shape
    rows = queries.shape[0]
    rows_spec = pl.BlockSpec((rows, feature), lambda h: (0, h))
    weight_spec = pl.BlockSpec((1, feature, feature), lambda h: (h, 0, 0))
    return pl.pallas_call(
        apply_body,
        grid=(heads,),
        in_specs=[rows_spec] + [weight_spec] * KINDS,
        out_specs=rows_spec,
        out_shape=jax.ShapeDtypeStruct(queries.shape, jnp.bfloat16),
        compiler_params=pltpu.CompilerParams(vmem_limit_bytes=VMEM_LIMIT),
        name="fast_apply",
    )(queries, *weights)


def projection_body(rows_ref, w_ref, o_ref):
    o_ref[...] = dot_on(rows_ref[...], w_ref[...], 1, 0).astype(o_ref.dtype)


def projection_call(fast_rows, w_out):
    rows, depth = fast_rows.shape
    width = w_out.shape[1]
    tile = next(size for size in (512, 256, 128, width) if width % size == 0)
    return pl.pallas_call(
        projection_body,
        grid=(width // tile,),
        in_specs=[
            pl.BlockSpec((rows, depth), lambda j: (0, 0)),
            pl.BlockSpec((depth, tile), lambda j: (0, j)),
        ],
        out_specs=pl.BlockSpec((rows, tile), lambda j: (0, j)),
        out_shape=jax.ShapeDtypeStruct((rows, width), jnp.bfloat16),
        compiler_params=pltpu.CompilerParams(vmem_limit_bytes=VMEM_LIMIT),
        name="projection",
    )(fast_rows, w_out)


def attention_body(q_ref, kp_ref, vp_ref, k_ref, v_ref, o_ref):
    rows = q_ref.shape[0]
    first = lax.axis_index("seq") == 0
    row = lax.broadcasted_iota(jnp.int32, (rows, rows), 0)
    col = lax.broadcasted_iota(jnp.int32, (rows, rows), 1)
    column_floor = jnp.where(first, rows, 0)
    prior_ok = (col > row) & (col >= column_floor)
    own_ok = col <= row
    for head in range(q_ref.shape[1] // AD):
        lanes = slice(head * AD, (head + 1) * AD)
        queries = q_ref[:, lanes]
        prior = dot_on(queries, kp_ref[:, lanes], 1, 1) * AD ** (-0.5)
        own = dot_on(queries, k_ref[:, lanes], 1, 1) * AD ** (-0.5)
        prior = jnp.where(prior_ok, prior, -1e30)
        own = jnp.where(own_ok, own, -1e30)
        top = jnp.max(jnp.maximum(prior, own), axis=-1, keepdims=True)
        prior = jnp.exp(prior - top)
        own = jnp.exp(own - top)
        scale = 1.0 / jnp.sum(prior + own, axis=-1, keepdims=True)
        prior = (prior * scale).astype(jnp.bfloat16)
        own = (own * scale).astype(jnp.bfloat16)
        o_ref[:, lanes] = (
            dot_on(prior, vp_ref[:, lanes], 1, 0) + dot_on(own, v_ref[:, lanes], 1, 0)
        ).astype(o_ref.dtype)


def attention_call(queries, prior_keys, prior_values, keys_in, values_in):
    rows, width = queries.shape
    heads = width // AD
    group = 2 * AD if heads % 2 == 0 else AD
    spec = pl.BlockSpec((rows, group), lambda h: (0, h))
    return pl.pallas_call(
        attention_body,
        grid=(width // group,),
        in_specs=[spec] * 5,
        out_specs=spec,
        out_shape=jax.ShapeDtypeStruct(queries.shape, jnp.float32),
        compiler_params=pltpu.CompilerParams(vmem_limit_bytes=VMEM_LIMIT),
        name="attention",
    )(queries, prior_keys, prior_values, keys_in, values_in)


def newton_step(y_ref, kind):
    first, second, third = NEWTON_COEFFS
    matrix = y_ref[kind]
    gram = dot_on(matrix, matrix, 1, 1).astype(jnp.bfloat16)
    square = dot_on(gram, gram, 1, 0)
    poly = (second * gram.astype(jnp.float32) + third * square).astype(jnp.bfloat16)
    y_ref[kind] = (first * matrix.astype(jnp.float32) + dot_on(poly, matrix, 1, 0)).astype(
        jnp.bfloat16
    )


def update_body(span, seq_count, g_ref, wg_ref, wu_ref, wd_ref, *refs):
    last = span == SPANS - 1
    outs = refs[: 1 if last else KINDS]
    (near, total, far, x_ref, y_ref, new_ref) = refs[len(outs) : len(outs) + 6]
    (send_near, recv_near, send_far, recv_far, pair_sem, send_out, recv_out, ready) = refs[
        len(outs) + 6 :
    ]
    w_refs = (wg_ref, wu_ref, wd_ref)
    per_span = seq_count // SPANS
    chips = per_span // 2
    feature = g_ref.shape[-1]
    half = feature // 2
    me = lax.axis_index("seq")
    my_span = me // per_span
    place = me % per_span
    chip = place // 2
    core = place % 2
    mate = me + 1 - 2 * core
    column = chip % 2
    layer = chip // 2
    own_rows = pl.ds(pl.multiple_of(core * half, half), half)
    mate_rows = pl.ds(pl.multiple_of((1 - core) * half, half), half)
    in_span = my_span == span

    def remote(src, dst, send, recv, device):
        return pltpu.make_async_remote_copy(
            src_ref=src, dst_ref=dst, send_sem=send, recv_sem=recv,
            device_id={"seq": device}, device_id_type=MESH,
        )

    def at_place(which_span, which_chip):
        return which_span * per_span + 2 * which_chip + core

    barrier = pltpu.get_barrier_semaphore()
    if last:
        for step in range(1, seq_count):
            pl.semaphore_signal(
                barrier, inc=1, device_id={"seq": (me + step) % seq_count}, device_id_type=MESH
            )
        pl.semaphore_wait(barrier, seq_count - 1)
    else:
        for step in range(1, per_span):
            peer = my_span * per_span + (place + step) % per_span
            pl.semaphore_signal(barrier, inc=1, device_id={"seq": peer}, device_id_type=MESH)

        @pl.when(in_span)
        def _():
            pl.semaphore_signal(
                barrier, inc=1, device_id={"seq": at_place(span + 1, column)}, device_id_type=MESH
            )

        @pl.when(in_span)
        def _():
            pl.semaphore_wait(barrier, per_span - 1)

        @pl.when(jnp.logical_not(in_span) & (layer == 0))
        def _():
            pl.semaphore_wait(barrier, per_span - 1 + 2)

        @pl.when(jnp.logical_not(in_span) & (layer != 0))
        def _():
            pl.semaphore_wait(barrier, per_span - 1)

    @pl.when(in_span)
    def _():
        targets = [(chip + step) % chips for step in range(1, chips)] + [chip]

        def near_copy(kind, slot):
            return remote(
                g_ref.at[kind, targets[slot], mate_rows], near.at[kind, slot],
                send_near.at[kind, slot], recv_near.at[kind, slot], mate,
            )

        def far_copy(kind, slot):
            return remote(
                total.at[kind, slot], far.at[kind, slot],
                send_far.at[kind, slot], recv_far.at[kind, slot], at_place(span, targets[slot]),
            )

        def pair_copy(kind):
            return remote(
                x_ref.at[kind, own_rows], x_ref.at[kind, own_rows],
                pair_sem.at[0, kind], pair_sem.at[1, kind], mate,
            )

        for kind in range(KINDS):
            for slot in range(chips):
                near_copy(kind, slot).start()
        for kind in range(KINDS):
            for slot, target in enumerate(targets[:-1]):
                near_copy(kind, slot).wait_recv()
                total[kind, slot] = (
                    g_ref[kind, target, own_rows].astype(jnp.float32)
                    + near[kind, slot].astype(jnp.float32)
                ).astype(jnp.bfloat16)
                far_copy(kind, slot).start()
            near_copy(kind, chips - 1).wait_recv()
        if not last:
            for kind in range(KINDS):
                outs[kind][...] = w_refs[kind][...]
        out_copies = []
        for kind in range(KINDS):
            summed = g_ref[kind, chip, own_rows].astype(jnp.float32)
            summed = summed + near[kind, chips - 1].astype(jnp.float32)
            for slot in range(chips - 1):
                far_copy(kind, slot).wait_recv()
                summed = summed + far[kind, slot].astype(jnp.float32)
            x_ref[kind, own_rows] = summed.astype(jnp.bfloat16)
            pair_copy(kind).start()
            pair_copy(kind).wait()
            gathered = x_ref[kind].astype(jnp.float32)
            norm = jnp.sqrt(jnp.sum(gathered * gathered, keepdims=True) + 1e-06)
            y_ref[kind] = (gathered / norm).astype(jnp.bfloat16)

            @pl.loop(0, NS_STEPS)
            def _(step):
                newton_step(y_ref, kind)

            unmoved = w_refs[kind][chip].astype(jnp.float32)
            moved = unmoved - y_ref[kind].astype(jnp.float32)
            target = jnp.sqrt(jnp.sum(unmoved * unmoved, axis=0, keepdims=True) + 1e-06)
            current = jnp.sqrt(jnp.sum(moved * moved, axis=0, keepdims=True) + 1e-06)
            new_ref[kind] = (moved * (target / current)).astype(jnp.bfloat16)
            if not last:
                if kind == 0:
                    pl.semaphore_wait(ready, 1)
                copy = remote(
                    new_ref.at[kind, own_rows], outs[kind].at[chip, own_rows],
                    send_out.at[0, kind, 0], recv_out.at[core, kind, chip],
                    at_place(span + 1, column),
                )
                copy.start()
                out_copies.append(copy)
                continue
            share = feature // seq_count
            chip_count = seq_count // 2
            for step in range(1, chip_count):
                device = 2 * ((me // 2 + step) % chip_count) + core
                there = pl.ds(pl.multiple_of(device * share, share), share)
                copy = remote(
                    new_ref.at[kind, there], outs[0].at[kind, chip],
                    send_out.at[kind, step], recv_out.at[kind, chip], device,
                )
                copy.start()
                out_copies.append(copy)
            here = pl.ds(pl.multiple_of(me * share, share), share)
            outs[0][kind, chip] = new_ref[kind, here]
        for copy in out_copies:
            copy.wait_send()
        for kind in range(KINDS):
            for slot in range(chips):
                near_copy(kind, slot).wait_send()
            for slot in range(chips - 1):
                far_copy(kind, slot).wait_send()

    if last:
        for owner in range(chips):
            @pl.when(jnp.logical_not(in_span & (chip == owner)))
            def _():
                for kind in range(KINDS):
                    remote(
                        new_ref.at[kind, pl.ds(0, feature // seq_count)],
                        outs[0].at[kind, owner],
                        send_out.at[kind, 0], recv_out.at[kind, owner], mate,
                    ).wait_recv()
        return

    @pl.when(jnp.logical_not(in_span))
    def _():
        @pl.when(layer == 0)
        def _():
            for owner_layer in range(2):
                pl.semaphore_signal(
                    ready, inc=1, device_id={"seq": at_place(span, 2 * owner_layer + column)},
                    device_id_type=MESH,
                )

        def passing(kind, owner, lane, device):
            block = outs[kind].at[owner, own_rows]
            return remote(
                block, block, send_out.at[lane, kind, owner], recv_out.at[core, kind, owner], device
            )

        chunks = [(kind, owner_layer) for kind in range(KINDS) for owner_layer in (1, 0)]
        across = at_place(my_span, 2 * layer + 1 - column)
        beyond = at_place(my_span, 2 + column)

        def cross_chunk(kind, owner_layer):
            to_mate = passing(kind, 2 * owner_layer + 1 - column, 0, mate)
            to_mate.wait_recv()
            to_mate.start()

        for number, (kind, owner_layer) in enumerate(chunks):
            owner = 2 * owner_layer + column
            passing(kind, owner, 0, mate).wait_recv()

            @pl.when(layer == 0)
            def _():
                passing(kind, owner, 2, beyond).start()

            passing(kind, owner, 1, across).start()
            passing(kind, owner, 0, mate).start()
            if number:
                cross_chunk(*chunks[number - 1])
        cross_chunk(*chunks[-1])
        for kind, owner_layer in chunks:
            for owner in (2 * owner_layer + column, 2 * owner_layer + 1 - column):
                other = outs[kind].at[owner, mate_rows]
                remote(
                    other, other, send_out.at[0, kind, owner],
                    recv_out.at[1 - core, kind, owner], mate,
                ).wait_recv()
                passing(kind, owner, 0, mate).wait_send()
            owner = 2 * owner_layer + column
            passing(kind, owner, 1, across).wait_send()

            @pl.when(layer == 0)
            def _():
                passing(kind, owner, 2, beyond).wait_send()


def update_call(span, seq_count, grads, weights):
    last = span == SPANS - 1
    _, heads, feature, _ = grads.shape
    chips = seq_count // SPANS // 2
    half = feature // 2
    vmem = pl.BlockSpec(memory_space=pltpu.VMEM)
    if last:
        out_shape = [
            jax.ShapeDtypeStruct((KINDS, heads, feature // seq_count, feature), jnp.bfloat16)
        ]
        out_sems = [
            pltpu.SemaphoreType.DMA((KINDS, seq_count // 2)),
            pltpu.SemaphoreType.DMA((KINDS, chips)),
        ]
    else:
        out_shape = [jax.ShapeDtypeStruct(weights[0].shape, jnp.bfloat16)] * KINDS
        out_sems = [
            pltpu.SemaphoreType.DMA((3, KINDS, heads)),
            pltpu.SemaphoreType.DMA((2, KINDS, heads)),
        ]
    return pl.pallas_call(
        functools.partial(update_body, span, seq_count),
        out_shape=out_shape,
        in_specs=[vmem] * 4,
        out_specs=[vmem] * len(out_shape),
        scratch_shapes=[
            pltpu.VMEM((KINDS, chips, half, feature), jnp.bfloat16),
            pltpu.VMEM((KINDS, chips - 1, half, feature), jnp.bfloat16),
            pltpu.VMEM((KINDS, chips - 1, half, feature), jnp.bfloat16),
            pltpu.VMEM((KINDS, feature, feature), jnp.bfloat16),
            pltpu.VMEM((KINDS, feature, feature), jnp.bfloat16),
            pltpu.VMEM((KINDS, feature, feature), jnp.bfloat16),
            pltpu.SemaphoreType.DMA((KINDS, chips)),
            pltpu.SemaphoreType.DMA((KINDS, chips)),
            pltpu.SemaphoreType.DMA((KINDS, chips - 1)),
            pltpu.SemaphoreType.DMA((KINDS, chips - 1)),
            pltpu.SemaphoreType.DMA((2, KINDS)),
            *out_sems,
            pltpu.SemaphoreType.REGULAR,
        ],
        compiler_params=pltpu.CompilerParams(
            collective_id=span, has_side_effects=True, vmem_limit_bytes=VMEM_LIMIT
        ),
        cost_estimate=pl.CostEstimate(
            flops=60_000_000_000, bytes_accessed=2**28, transcendentals=0
        ),
        name=f"update{span}",
    )(grads, *weights)


def owned_on_device(
    fast_q, fast_k, fast_v, rates, w_gate, w_up, w_down, w_out, att_q, att_k, att_v
):
    seq_count = lax.axis_size("seq")
    early = lax.axis_index("seq") < seq_count // SPANS
    start = (w_gate, w_up, w_down)
    rate_cols = rates[:, :, None]
    heads, feature, _ = w_gate.shape
    count = seq_count // SPANS

    def prior_of(blocks, low, high):
        route = [(i - 1, i) for i in range(max(low, 1), high)]
        return tuple(lax.ppermute(block, "seq", route) for block in blocks)

    def attention(prior):
        return attention_call(att_q, *prior, att_k, att_v)

    def slopes(weights):
        return gradient_call(weights, fast_k, fast_v, rate_cols)

    grads = lax.cond(
        early,
        lambda: slopes(start),
        lambda: jnp.zeros((KINDS, heads, feature, feature), jnp.bfloat16),
    )
    prior = prior_of((att_k, att_v), count, seq_count)
    waited = lax.cond(
        early, lambda: jnp.zeros(att_q.shape, jnp.float32), lambda: attention(prior)
    )
    grads, waited = lax.optimization_barrier((grads, waited))
    weights = update_call(0, seq_count, grads, start)
    weights, later = lax.optimization_barrier((weights, (att_k, att_v)))
    early_prior = prior_of(later, 0, count)
    grads, attended = lax.cond(
        early,
        lambda: (grads, attention(early_prior)),
        lambda: (slopes(weights), waited),
    )
    fast_rows = apply_call(weights, fast_q)
    partial_out = projection_call(fast_rows, w_out)
    grads, partial_out = lax.optimization_barrier((grads, partial_out))
    fast_sum = lax.psum_scatter(partial_out, "head", scatter_dimension=1, tiled=True)
    (final_weights,) = update_call(1, seq_count, grads, weights)
    return ((attended + fast_sum.astype(jnp.float32)).astype(jnp.bfloat16), final_weights)


def solution(mesh):
    in_specs = (
        P("seq", "head"),
        P("seq", "head"),
        P("seq", "head"),
        P("head", "seq"),
        P("head", None, None),
        P("head", None, None),
        P("head", None, None),
        P("head", None),
        P("seq", "head"),
        P("seq", "head"),
        P("seq", "head"),
    )
    out_specs = (P("seq", "head"), P(None, "head", "seq", None))
    owned = mesh.shape["seq"] == 4 * 2 * SPANS

    def either(*arrays):
        held = arrays[4].shape[0] == mesh.shape["seq"] // (2 * SPANS)
        return (owned_on_device if owned and held else on_device)(*arrays)

    return jax.shard_map(
        either, mesh=mesh, in_specs=in_specs, out_specs=out_specs, check_vma=False
    )
```
